32 devices in a mesh: groups: 2 (over y), rows: 16 (over z, x, core).
Axes of the slice: x: 2, y: 2, z: 4, core: 2. Of those that a mesh axis runs over, the one named last changes fastest.
Arguments:
- tile_values: float32 [5120, 128, 128], P(('groups', 'rows')), parts along dimension 0, may hold values from 0.01 to 1
- tile_row: int32 [5120], P(('groups', 'rows')), parts along dimension 0, may hold values from 0 to 127, as said below
- tile_col: int32 [5120], P(('groups', 'rows')), parts along dimension 0, may hold values from 0 to 127, as said below
- row_count: int32 [256], P(('groups', 'rows')), parts along dimension 0, may hold values from 1 to 24, as said below
- start_basis: float32 [24, 32768], P(None, ('groups', 'rows')), parts along dimension 1, may hold values from -6 to 6
Outputs:
- right_basis: float32 [24, 32768], P(None, ('groups', 'rows')), parts along dimension 1
The draws below stay inside these ranges and needn't reach their ends.
There are 2 independent parts, one for each index of `groups`. The reference program is written for one: setup_inputs(seed, part) draws one part's arguments, and reference() takes and returns one part's arrays. A program takes and returns all parts, laid end to end along the dimension named above; each array names one. Nothing has to cross between parts.
Inputs may be any that keep to these rules, and one draw needn't show every extreme that they name: `tile_row`: each device's slots hold its 8 block rows in order, row_count of a row consecutive slots for it, then empty slots that carry the device's last row. `tile_col`: within 16 of the slot's row; each row's slots name its own index once and no index twice; empty slots name their row's own index. `row_count`: the counts of one device's rows sum to at most 160, which some device reaches.
All inputs are finite; a program needn't handle non-finite values.
Results may differ from the reference program's by a relative error of at most 0.0003.
Values sent between devices are 32-bit elements; how exact they have to be, the bound alone decides.
A program may use at most 64 MiB of HBM per device.

```python
import math
import jax
import jax.numpy as jnp
from jax import lax

TILE = 128
K = 24
ROWS_DEV = 8
MOST_ROW = 24
ITERS = 2
REACH = 16
TILE_DEV = 160
NBR = 128
NBOX = 16384
N_TILES = 2560
N_ROWS = 16


def tile_plan(key):
    ndevices = NBR // ROWS_DEV
    key_extra, key_full, key_order = jax.random.split(key, 3)
    extra = jax.random.randint(key_extra, (ndevices, ROWS_DEV), 0, MOST_ROW).astype(jnp.int32)
    global_rows = jnp.arange(NBR, dtype=jnp.int32).reshape(ndevices, ROWS_DEV)
    avail = jnp.minimum(global_rows, REACH) + jnp.minimum(NBR - 1 - global_rows, REACH)
    full_dev = jax.random.randint(key_full, (), 2, ndevices - 2).astype(jnp.int32)
    extra = jnp.where(jnp.arange(ndevices, dtype=jnp.int32)[:, None] == full_dev, MOST_ROW - 1, extra)
    extra = jnp.minimum(extra, avail)
    spare = TILE_DEV - ROWS_DEV
    before = jnp.cumsum(extra, axis=1) - extra
    extra = jnp.clip(spare - before, 0, extra)
    counts = (1 + extra).astype(jnp.int32)
    starts = jnp.cumsum(counts, axis=1) - counts
    totals = jnp.sum(counts, axis=1)
    slot_ids = jnp.arange(TILE_DEV, dtype=jnp.int32)
    local_row = jnp.sum((starts[:, None, :] <= slot_ids[None, :, None]).astype(jnp.int32), axis=2) - 1
    live_slot = slot_ids[None, :] < totals[:, None]
    local_row = jnp.where(live_slot, local_row, ROWS_DEV - 1).astype(jnp.int32)
    position = jnp.where(live_slot, slot_ids[None, :] - jnp.take_along_axis(starts, local_row, axis=1), 0)
    slot_rows = global_rows[:, :1] + local_row
    span_width = 2 * REACH
    candidates = jnp.concatenate([jnp.arange(-REACH, 0, dtype=jnp.int32), jnp.arange(1, REACH + 1, dtype=jnp.int32)])
    target = jnp.arange(NBR, dtype=jnp.int32)[:, None] + candidates[None, :]
    inside = (target >= 0) & (target < NBR)
    scores = jax.random.randint(key_order, (NBR, span_width), 0, 1 << 20).astype(jnp.int32) * span_width
    scores = scores + jnp.arange(span_width, dtype=jnp.int32)[None, :]
    scores = jnp.where(inside, scores, scores + (1 << 30))
    order = jnp.argsort(scores, axis=1, stable=True)
    chosen = jnp.take_along_axis(jnp.broadcast_to(candidates, (NBR, span_width)), order, axis=1)[:, :MOST_ROW - 1]
    offsets = jnp.concatenate([jnp.zeros((NBR, 1), jnp.int32), chosen], axis=1)
    flat_rows = slot_rows.reshape(-1).astype(jnp.int32)
    flat_cols = flat_rows + offsets[flat_rows, position.reshape(-1)]
    return (counts.reshape(-1), flat_rows, flat_cols.astype(jnp.int32))


def draw_tile_row(key, part):
    plan = tile_plan(key)
    return plan[1]


def draw_tile_col(key, part):
    plan = tile_plan(key)
    return plan[2]


def draw_row_count(key, part):
    plan = tile_plan(key)
    return plan[0]


def level_of(own_key, extent, cuts, smallest, largest):
    def one(dim, shards_of):
        steps = jax.random.uniform(jax.random.fold_in(jax.random.fold_in(own_key, 6), dim), (shards_of,), jnp.float32, smallest / len(cuts), largest / len(cuts))
        return jnp.repeat(jnp.exp(steps), extent[dim] // shards_of).reshape((-1,) + (1,) * (len(extent) - dim - 1))

    factor_of = one(*cuts[0])
    for cut in cuts[1:]:
        factor_of = factor_of * one(*cut)
    return factor_of


def gaussian(stream_key, dims, deviation, limit, pieces=(), kind=jnp.bfloat16):
    level = level_of(stream_key, dims, pieces, -0.22, 0.18) if pieces else 1.0
    values = jax.random.normal(stream_key, dims, jnp.float32) * deviation * level
    return jnp.minimum(jnp.maximum(values, -limit), limit).astype(kind)


def setup_inputs(seed: int = 0, part: int = 0) -> dict:
    key_of = jax.random.split(jax.random.key(seed), 6)
    own_keys = jax.random.split(jax.random.fold_in(key_of[5], part), 6)
    tile_values = jnp.clip(jnp.exp(math.log(1.0) - 4.6051702 * jax.random.uniform(own_keys[0], (N_TILES, TILE, TILE), jnp.float32) ** level_of(own_keys[0], (N_TILES, TILE, TILE), ((0, 16),), -0.2, 0.2)), 0.01, 1.0)
    tile_row = draw_tile_row(jax.random.fold_in(jax.random.fold_in(key_of[5], part), 71), part)
    tile_col = draw_tile_col(jax.random.fold_in(jax.random.fold_in(key_of[5], part), 71), part)
    row_count = draw_row_count(jax.random.fold_in(jax.random.fold_in(key_of[5], part), 71), part)
    start_basis = gaussian(own_keys[4], (K, NBOX), 1.0, 6.0, ((1, 16),), jnp.float32)
    return {"tile_values": tile_values, "tile_row": tile_row, "tile_col": tile_col, "row_count": row_count, "start_basis": start_basis}


def reference(tile_values, tile_row, tile_col, row_count, start_basis):
    high = lax.Precision.HIGHEST
    slot_ids = jnp.arange(tile_values.shape[0], dtype=jnp.int32)
    totals = lax.optimization_barrier(jnp.sum(row_count.reshape(N_ROWS, ROWS_DEV), axis=1))
    live_slot = (slot_ids % TILE_DEV < totals[slot_ids // TILE_DEV]).astype(tile_values.dtype)
    row_mass = jax.ops.segment_sum(lax.optimization_barrier(jnp.sum(tile_values, axis=2)) * live_slot[:, None], tile_row, num_segments=NBR)
    col_mass = jax.ops.segment_sum(lax.optimization_barrier(jnp.sum(tile_values, axis=1)) * live_slot[:, None], tile_col, num_segments=NBR)
    all_mass = jnp.sum(col_mass)
    unit_vec = jnp.sqrt(col_mass / all_mass).reshape(-1)
    row_scale = 1.0 / jnp.sqrt(row_mass)
    col_scale = 1.0 / jnp.sqrt(col_mass)
    blocks = start_basis.reshape(K, NBR, TILE).transpose(1, 0, 2)
    orthonormal = start_basis
    for step in range(ITERS):
        scaled = blocks * col_scale[:, None, :]
        forward = jnp.einsum('sij,skj->ski', tile_values, scaled[tile_col], precision=high) * live_slot[:, None, None]
        image_rows = jax.ops.segment_sum(forward, tile_row, num_segments=NBR) * row_scale[:, None, :]
        weighted = image_rows * row_scale[:, None, :]
        back_prod = jnp.einsum('sij,ski->skj', tile_values, weighted[tile_row], precision=high) * live_slot[:, None, None]
        folded = jax.ops.segment_sum(back_prod, tile_col, num_segments=NBR) * col_scale[:, None, :]
        flat = folded.transpose(1, 0, 2).reshape(K, NBOX)
        along_unit = jnp.dot(flat, unit_vec, precision=high)
        cleaned = flat - along_unit[:, None] * unit_vec[None, :]
        gram_matrix = jnp.dot(cleaned, cleaned.T, precision=high)
        factor = jnp.linalg.cholesky(gram_matrix)
        orthonormal = lax.linalg.triangular_solve(factor, cleaned, left_side=True, lower=True)
        blocks = orthonormal.reshape(K, NBR, TILE).transpose(1, 0, 2)
    return orthonormal * math.sqrt(NBOX)
```

```python
import functools
import math

import jax
import jax.numpy as jnp
from jax import lax
from jax.experimental import pallas as pl
from jax.experimental.pallas import tpu as pltpu
from jax.sharding import PartitionSpec as P

MOST_ROW = 24
MESH = pl.DeviceIdType.MESH
OFFSETS = (-2, -1, 1, 2)
HIGH = lax.Precision.HIGHEST
NT = (((1,), (1,)), ((), ()))
NN = (((1,), (0,)), ((), ()))
F32 = jnp.float32
BF16 = jnp.bfloat16


def split(value):
    hi = value.astype(BF16).astype(F32)
    return hi, value - hi


def kernel(
    count, near, slots, rows, vectors, tlen, chunks,
    tab, basis, tiles_hbm, out,
    tiles, t_hi, t_lo, c_part, prod, v_win, v_win2, s_win, lhs_win, lhs_row,
    colw, col_in, z_part, z_in, z_own, zext, ar_out, ar_in,
    tile_sem, x_send, x_recv, a_send, a_recv,
):
    me = lax.axis_index("rows")
    far = count // near
    win = 5 * rows
    half = vectors + 8
    col_at, row_at = 0, slots
    cmap_at = 2 * slots
    rmap_at = cmap_at + win * rows
    per = slots // chunks

    tile_copies = []
    for c in range(chunks):
        part = pl.ds(c * per, per)
        copy = pltpu.make_async_copy(tiles_hbm.at[part], tiles.at[part], tile_sem.at[c])
        copy.start()
        tile_copies.append(copy)

    valid = [jnp.logical_and(me + d >= 0, me + d < count) for d in OFFSETS]
    stage_pos = (me % near, me // near)
    stage_len = (near, far)

    def partner(stage, j):
        if stage == 0:
            return (me // near) * near + (me % near + j) % near
        return ((me // near + j) % far) * near + me % near

    barrier = pltpu.get_barrier_semaphore()
    greeted = jnp.int32(near - 1 + far - 1)
    for d, ok in zip(OFFSETS, valid):
        greeted = greeted + ok.astype(jnp.int32)

        @pl.when(ok)
        def _(d=d):
            pl.semaphore_signal(barrier, inc=1, device_id={"rows": me + d}, device_id_type=MESH)

    for stage in (0, 1):
        for j in range(1, stage_len[stage]):
            pl.semaphore_signal(
                barrier, inc=1, device_id={"rows": partner(stage, j)}, device_id_type=MESH
            )

    for b in range(rows):
        v_win[2 * rows + b] = basis[:, b * tlen : (b + 1) * tlen]
    c_part[slots] = jnp.zeros((8, tlen), F32)
    prod[slots] = jnp.zeros((half, tlen), F32)
    zext[...] = jnp.zeros_like(zext)

    def neighbour(which, i, source, target):
        return pltpu.make_async_remote_copy(
            src_ref=source(OFFSETS[i]),
            dst_ref=target(OFFSETS[i]),
            send_sem=x_send.at[which, i],
            recv_sem=x_recv.at[which, i],
            device_id={"rows": me + OFFSETS[i]},
            device_id_type=MESH,
        )

    def send(which, source, target):
        for i in (0, 3, 1, 2):
            @pl.when(valid[i])
            def _(i=i):
                neighbour(which, i, source, target).start()

    def finish(which, source, target):
        for i in range(4):
            @pl.when(valid[i])
            def _(i=i):
                neighbour(which, i, source, target).wait_send()

            @pl.when(valid[3 - i])
            def _(i=i):
                neighbour(which, i, source, target).wait_recv()

    def own_v(d):
        return v_win.at[pl.ds(2 * rows, rows)]

    def to_v(d):
        return v_win.at[pl.ds((2 - d) * rows, rows)]

    def own_v2(d):
        return v_win2.at[pl.ds(2 * rows, rows)]

    def to_v2(d):
        return v_win2.at[pl.ds((2 - d) * rows, rows)]

    def own_s(d):
        return s_win.at[pl.ds(2 * rows, rows)]

    def to_s(d):
        return s_win.at[pl.ds((2 - d) * rows, rows)]

    def part_c(d):
        return colw.at[2 + d]

    def to_c(d):
        return col_in.at[OFFSETS.index(d)]

    def mass_chunk(c):
        tile_copies[c].wait()

        @pl.loop(c * per, (c + 1) * per, unroll=4)
        def _(s):
            tile = tiles[s]
            hi = tile.astype(BF16)
            t_hi[s] = hi
            t_lo[s] = (tile - hi.astype(F32)).astype(BF16)
            c_part[s] = jnp.sum(tile.reshape(tlen // 8, 8, tlen), axis=0)

    mass_chunk(0)
    pl.semaphore_wait(barrier, greeted)
    send(0, own_v, to_v)
    for c in range(1, chunks):
        mass_chunk(c)

    @pl.loop(0, 5)
    def _(w):
        lines = []
        for b in range(rows):
            at = cmap_at + (w * rows + b) * rows
            total = c_part[tab[at]]
            for r in range(1, rows):
                total = total + c_part[tab[at + r]]
            lines.append(jnp.sum(total, axis=0, keepdims=True))
        colw[w] = jnp.concatenate(lines, axis=0)

    send(1, part_c, to_c)
    finish(1, part_c, to_c)
    for i in range(4):
        @pl.when(valid[3 - i])
        def _(i=i):
            colw[2] = colw[2] + col_in[i]

    mass = colw[2]
    col_scale = 1.0 / jnp.sqrt(mass)
    root = jnp.sqrt(mass)
    s_win[2 * rows : 3 * rows] = col_scale
    send(2, own_s, to_s)

    for b in range(rows):
        zext[vectors : vectors + 1, b * tlen : (b + 1) * tlen] = root[b : b + 1]

    def reduce_copy(which, stage, j):
        return pltpu.make_async_remote_copy(
            src_ref=ar_out.at[which, stage],
            dst_ref=ar_in.at[which, stage, j - 1],
            send_sem=a_send.at[which, stage, j - 1],
            recv_sem=a_recv.at[which, stage, j - 1],
            device_id={"rows": partner(stage, j)},
            device_id_type=MESH,
        )

    def reduce_send(which, stage, value):
        ar_out[which, stage] = value
        for j in range(1, stage_len[stage]):
            reduce_copy(which, stage, j).start()

    def reduce_wait(which, stage):
        total = ar_out[which, stage]
        for j in range(1, stage_len[stage]):
            copy = reduce_copy(which, stage, j)
            copy.wait_send()
            copy.wait_recv()
            total = total + ar_in[which, stage, j - 1]
        return total

    def gram_packed():
        value = zext[...]
        gram = lax.dot_general(value[0:32], value, NT, precision=HIGH, preferred_element_type=F32)
        packed = gram[0:8]
        for b in range(1, 4):
            packed = packed + pltpu.roll(gram[8 * b : 8 * b + 8], 32 * b, 1)
        return packed

    lane = lax.broadcasted_iota(jnp.int32, (vectors, 128), 1)
    line = lax.broadcasted_iota(jnp.int32, (vectors, 128), 0)

    def unpack(packed):
        parts = [packed] + [pltpu.roll(packed, 128 - 32 * b, 1) for b in (1, 2)]
        gram = jnp.concatenate(parts, axis=0)
        last = pltpu.roll(packed, 32, 1)
        unit_row = last[0:1]
        mass_all = last[0:1, vectors : vectors + 1]
        along = gram[:, vectors : vectors + 1] / mass_all
        return gram, unit_row, along

    def inverse_factor(gram, unit_row, along):
        work = jnp.where(lane < vectors, gram - along * unit_row, 0.0)
        work = jnp.where(lane == line + 32, 1.0, work)
        for j in range(vectors):
            top = work[j : j + 1]
            ratio = work[:, j : j + 1] / top[:, j : j + 1]
            work = work - jnp.where(line[:, 0:1] > j, ratio, 0.0) * top
        diag = jnp.sum(jnp.where(lane == line, work, 0.0), axis=1, keepdims=True)
        work = work * (1.0 / jnp.sqrt(diag))
        return jnp.where(lane < vectors, pltpu.roll(work, 96, 1), 0.0)

    def mix(factor, value):
        padded = jnp.concatenate([value, jnp.zeros((128 - vectors, tlen), F32)], axis=0)
        return lax.dot_general(factor, padded, NN, precision=HIGH, preferred_element_type=F32)

    for b in range(rows):
        zext[0:vectors, b * tlen : (b + 1) * tlen] = v_win[2 * rows + b]
    reduce_send(0, 0, gram_packed())

    ones8 = jnp.ones((8, tlen), F32)
    zeros8 = jnp.zeros((8, tlen), F32)

    def left_side(value, extra):
        hi, lo = split(value)
        return jnp.concatenate([hi, extra, lo, zeros8], axis=0).astype(BF16)

    def forward():
        @pl.loop(0, slots, unroll=8)
        def _(s):
            left = lhs_win[tab[col_at + s]]
            big = lax.dot_general(left, t_hi[s], NT, preferred_element_type=F32)
            small = lax.dot_general(left[0:half], t_lo[s], NT, preferred_element_type=F32)
            prod[s] = big[0:half] + big[half:] + small

    def row_total(r):
        at = rmap_at + r * MOST_ROW
        total = prod[tab[at]]
        for p in range(1, MOST_ROW):
            total = total + prod[tab[at + p]]
        return total[0:vectors] * (1.0 / total[vectors : vectors + 1])

    def backward(step):
        @pl.loop(0, slots, unroll=8)
        def _(s):
            left = lhs_row[tab[row_at + s]]
            big = lax.dot_general(left, t_hi[s], NN, preferred_element_type=F32)
            small = lax.dot_general(left[0:half], t_lo[s], NN, preferred_element_type=F32)
            prod[s] = big[0:half] + big[half:] + small

        @pl.loop(0, win)
        def _(c):
            at = cmap_at + c * rows
            total = prod[tab[at], 0:vectors]
            for r in range(1, rows):
                total = total + prod[tab[at + r], 0:vectors]
            z_part[step, c] = total

    def exchange_z(step):
        def source(d):
            return z_part.at[step, pl.ds((2 + d) * rows, rows)]

        def target(d):
            return z_in.at[step, OFFSETS.index(d)]

        send(3 + step, source, target)
        finish(3 + step, source, target)
        z_own[...] = z_part[step, 2 * rows : 3 * rows]
        for i in range(4):
            @pl.when(valid[3 - i])
            def _(i=i):
                z_own[...] = z_own[...] + z_in[step, i]

    finish(0, own_v, to_v)
    finish(2, own_s, to_s)

    @pl.loop(0, win, unroll=4)
    def _(c):
        lhs_win[c] = left_side(v_win[c] * s_win[pl.ds(c, 1)], ones8)

    forward()
    reduce_send(0, 1, reduce_wait(0, 0))

    @pl.loop(0, rows)
    def _(r):
        lhs_row[r] = left_side(row_total(r), zeros8)

    backward(0)
    _, _, along = unpack(reduce_wait(0, 1))
    exchange_z(0)
    for b in range(rows):
        cleaned = z_own[b] * col_scale[b : b + 1] - along * root[b : b + 1]
        zext[0:vectors, b * tlen : (b + 1) * tlen] = cleaned
        v_win2[2 * rows + b] = cleaned * col_scale[b : b + 1]
    send(5, own_v2, to_v2)
    reduce_send(1, 0, gram_packed())
    finish(5, own_v2, to_v2)

    @pl.loop(0, win, unroll=4)
    def _(c):
        lhs_win[c] = left_side(v_win2[c], ones8)

    reduce_send(1, 1, reduce_wait(1, 0))
    forward()
    factor = inverse_factor(*unpack(reduce_wait(1, 1)))

    @pl.loop(0, rows)
    def _(r):
        lhs_row[r] = left_side(mix(factor, row_total(r)), zeros8)

    backward(1)
    exchange_z(1)
    for b in range(rows):
        zext[0:vectors, b * tlen : (b + 1) * tlen] = z_own[b] * col_scale[b : b + 1]
    reduce_send(2, 0, gram_packed())
    reduce_send(2, 1, reduce_wait(2, 0))
    gram, unit_row, along = unpack(reduce_wait(2, 1))
    factor = inverse_factor(gram, unit_row, along)
    factor = factor * math.sqrt(count * rows * tlen)
    for b in range(rows):
        cols = slice(b * tlen, (b + 1) * tlen)
        out[:, cols] = mix(factor, zext[0:vectors, cols] - along * root[b : b + 1])


def body(tile_values, tile_row, tile_col, row_count, start_basis):
    slots, tlen = tile_values.shape[:2]
    rows = row_count.shape[0]
    vectors = start_basis.shape[0]
    count = lax.axis_size("rows")
    near = 4 if count <= 16 else 8
    win = 5 * rows
    first = lax.axis_index("rows") * rows
    row_here = tile_row - first
    col_here = tile_col - (first - 2 * rows)
    slot = jnp.arange(slots, dtype=jnp.int32)
    live = slot < jnp.sum(row_count)
    place = jnp.where(live, col_here * rows + row_here, -1)
    cells = jnp.arange(win * rows, dtype=jnp.int32)
    col_map = jnp.min(jnp.where(place[None, :] == cells[:, None], slot[None, :], slots), axis=1)
    line = jnp.arange(rows, dtype=jnp.int32)
    starts = jnp.sum(jnp.where(line[None, :] < line[:, None], row_count[None, :], 0), axis=1)
    spot = jnp.arange(MOST_ROW, dtype=jnp.int32)
    row_map = jnp.where(
        spot[None, :] < row_count[:, None], starts[:, None] + spot[None, :], slots
    ).reshape(-1)
    table = jnp.concatenate([col_here, row_here, col_map, row_map]).astype(jnp.int32)
    chunks = 8
    most = max(near, count // near)
    half = vectors + 8
    vmem = pltpu.VMEM
    return pl.pallas_call(
        functools.partial(kernel, count, near, slots, rows, vectors, tlen, chunks),
        out_shape=jax.ShapeDtypeStruct(start_basis.shape, F32),
        in_specs=[
            pl.BlockSpec(memory_space=pltpu.SMEM),
            pl.BlockSpec(memory_space=pltpu.VMEM),
            pl.BlockSpec(memory_space=pl.ANY),
        ],
        out_specs=pl.BlockSpec(memory_space=pltpu.VMEM),
        scratch_shapes=[
            vmem((slots, tlen, tlen), F32),
            vmem((slots, tlen, tlen), BF16),
            vmem((slots, tlen, tlen), BF16),
            vmem((slots + 1, 8, tlen), F32),
            vmem((slots + 1, half, tlen), F32),
            vmem((win, vectors, tlen), F32),
            vmem((win, vectors, tlen), F32),
            vmem((win, tlen), F32),
            vmem((win, 2 * half, tlen), BF16),
            vmem((rows, 2 * half, tlen), BF16),
            vmem((5, rows, tlen), F32),
            vmem((4, rows, tlen), F32),
            vmem((2, win, vectors, tlen), F32),
            vmem((2, 4, rows, vectors, tlen), F32),
            vmem((rows, vectors, tlen), F32),
            vmem((128, rows * tlen), F32),
            vmem((3, 2, 8, 128), F32),
            vmem((3, 2, most, 8, 128), F32),
            pltpu.SemaphoreType.DMA((chunks,)),
            pltpu.SemaphoreType.DMA((6, 4)),
            pltpu.SemaphoreType.DMA((6, 4)),
            pltpu.SemaphoreType.DMA((3, 2, most)),
            pltpu.SemaphoreType.DMA((3, 2, most)),
        ],
        compiler_params=pltpu.CompilerParams(
            collective_id=0, has_side_effects=True, vmem_limit_bytes=48 * 1024 * 1024
        ),
    )(table, start_basis, tile_values)


def solution(mesh):
    placed = (
        P(("groups", "rows"), None, None),
        P(("groups", "rows")),
        P(("groups", "rows")),
        P(("groups", "rows")),
        P(None, ("groups", "rows")),
    )
    return jax.shard_map(
        body, mesh=mesh, in_specs=placed, out_specs=P(None, ("groups", "rows")), check_vma=False
    )
```

```python
import functools
import math

import jax
import jax.numpy as jnp
from jax import lax
from jax.experimental import pallas as pl
from jax.experimental.pallas import tpu as pltpu
from jax.sharding import PartitionSpec as P

MOST_ROW = 24
MESH = pl.DeviceIdType.MESH
OFFSETS = (-2, -1, 1, 2)
HIGH = lax.Precision.HIGHEST
NT = (((1,), (1,)), ((), ()))
NN = (((1,), (0,)), ((), ()))
F32 = jnp.float32
BF16 = jnp.bfloat16


def split(value):
    hi = value.astype(BF16).astype(F32)
    return hi, value - hi


def kernel(
    count, near, slots, rows, vectors, tlen, chunks,
    tab, basis, tiles_hbm, out,
    tiles, t_own, t_flip, c_part, prod, v_win, v_win2, s_win, lhs_win, lhs_row,
    row_inv, colw, col_in, z_part, z_in, z_own, zext, ar_out, ar_in,
    tile_sem, x_send, x_recv, a_send, a_recv,
):
    me = lax.axis_index("rows")
    far = count // near
    win = 5 * rows
    half = vectors + 8
    col_at, row_at = 0, slots
    cmap_at = 2 * slots
    rmap_at = cmap_at + win * rows
    per = slots // chunks

    tile_copies = []
    for c in range(chunks):
        part = pl.ds(c * per, per)
        copy = pltpu.make_async_copy(tiles_hbm.at[part], tiles.at[part], tile_sem.at[c])
        copy.start()
        tile_copies.append(copy)

    valid = [jnp.logical_and(me + d >= 0, me + d < count) for d in OFFSETS]
    stage_pos = (me % near, me // near)
    stage_len = (near, far)

    def partner(stage, j):
        if stage == 0:
            return (me // near) * near + (me % near + j) % near
        return ((me // near + j) % far) * near + me % near

    barrier = pltpu.get_barrier_semaphore()
    greeted = jnp.int32(near - 1 + far - 1)
    for d, ok in zip(OFFSETS, valid):
        greeted = greeted + ok.astype(jnp.int32)

        @pl.when(ok)
        def _(d=d):
            pl.semaphore_signal(barrier, inc=1, device_id={"rows": me + d}, device_id_type=MESH)

    for stage in (0, 1):
        for j in range(1, stage_len[stage]):
            pl.semaphore_signal(
                barrier, inc=1, device_id={"rows": partner(stage, j)}, device_id_type=MESH
            )

    for b in range(rows):
        v_win[2 * rows + b] = basis[:, b * tlen : (b + 1) * tlen]
    c_part[slots] = jnp.zeros((8, tlen), F32)
    prod[slots] = jnp.zeros((half, tlen), F32)
    zext[...] = jnp.zeros_like(zext)

    def neighbour(which, i, source, target):
        return pltpu.make_async_remote_copy(
            src_ref=source(OFFSETS[i]),
            dst_ref=target(OFFSETS[i]),
            send_sem=x_send.at[which, i],
            recv_sem=x_recv.at[which, i],
            device_id={"rows": me + OFFSETS[i]},
            device_id_type=MESH,
        )

    def send(which, source, target):
        for i in (0, 3, 1, 2):
            @pl.when(valid[i])
            def _(i=i):
                neighbour(which, i, source, target).start()

    def finish(which, source, target):
        for i in range(4):
            @pl.when(valid[i])
            def _(i=i):
                neighbour(which, i, source, target).wait_send()

            @pl.when(valid[3 - i])
            def _(i=i):
                neighbour(which, i, source, target).wait_recv()

    def own_v(d):
        return v_win.at[pl.ds(2 * rows, rows)]

    def to_v(d):
        return v_win.at[pl.ds((2 - d) * rows, rows)]

    def own_v2(d):
        return v_win2.at[pl.ds(2 * rows, rows)]

    def to_v2(d):
        return v_win2.at[pl.ds((2 - d) * rows, rows)]

    def own_s(d):
        return s_win.at[pl.ds(2 * rows, rows)]

    def to_s(d):
        return s_win.at[pl.ds((2 - d) * rows, rows)]

    def part_c(d):
        return colw.at[2 + d]

    def to_c(d):
        return col_in.at[OFFSETS.index(d)]

    def mass_chunk(c):
        tile_copies[c].wait()

        @pl.loop(c * per, (c + 1) * per, unroll=4)
        def _(s):
            tile = tiles[s]
            hi = tile.astype(BF16)
            t_own[s, 0:tlen] = hi
            t_own[s, tlen:] = (tile - hi.astype(F32)).astype(BF16)
            c_part[s] = jnp.sum(tile.reshape(tlen // 8, 8, tlen), axis=0)

    mass_chunk(0)
    pl.semaphore_wait(barrier, greeted)
    send(0, own_v, to_v)
    for c in range(1, chunks):
        mass_chunk(c)

    @pl.loop(0, 5)
    def _(w):
        lines = []
        for b in range(rows):
            at = cmap_at + (w * rows + b) * rows
            total = c_part[tab[at]]
            for r in range(1, rows):
                total = total + c_part[tab[at + r]]
            lines.append(jnp.sum(total, axis=0, keepdims=True))
        colw[w] = jnp.concatenate(lines, axis=0)

    def flip(begin, end):
        @pl.loop(begin, end, unroll=4)
        def _(s):
            t_flip[s, 0:tlen] = t_own[s, 0:tlen].T
            t_flip[s, tlen:] = t_own[s, tlen:].T

    send(1, part_c, to_c)
    flip(0, slots // 2)
    finish(1, part_c, to_c)
    for i in range(4):
        @pl.when(valid[3 - i])
        def _(i=i):
            colw[2] = colw[2] + col_in[i]

    mass = colw[2]
    col_scale = 1.0 / jnp.sqrt(mass)
    root = jnp.sqrt(mass)
    s_win[2 * rows : 3 * rows] = col_scale
    send(2, own_s, to_s)

    for b in range(rows):
        zext[vectors : vectors + 1, b * tlen : (b + 1) * tlen] = root[b : b + 1]

    def reduce_copy(which, stage, j):
        return pltpu.make_async_remote_copy(
            src_ref=ar_out.at[which, stage],
            dst_ref=ar_in.at[which, stage, j - 1],
            send_sem=a_send.at[which, stage, j - 1],
            recv_sem=a_recv.at[which, stage, j - 1],
            device_id={"rows": partner(stage, j)},
            device_id_type=MESH,
        )

    def reduce_send(which, stage, value):
        ar_out[which, stage] = value
        for j in range(1, stage_len[stage]):
            reduce_copy(which, stage, j).start()

    def reduce_wait(which, stage):
        total = ar_out[which, stage]
        for j in range(1, stage_len[stage]):
            copy = reduce_copy(which, stage, j)
            copy.wait_send()
            copy.wait_recv()
            total = total + ar_in[which, stage, j - 1]
        return total

    def gram_packed():
        value = zext[...]
        gram = lax.dot_general(value[0:32], value, NT, precision=HIGH, preferred_element_type=F32)
        packed = gram[0:8]
        for b in range(1, 4):
            packed = packed + pltpu.roll(gram[8 * b : 8 * b + 8], 32 * b, 1)
        return packed

    lane = lax.broadcasted_iota(jnp.int32, (vectors, 128), 1)
    line = lax.broadcasted_iota(jnp.int32, (vectors, 128), 0)

    def unpack(packed):
        parts = [packed] + [pltpu.roll(packed, 128 - 32 * b, 1) for b in (1, 2)]
        gram = jnp.concatenate(parts, axis=0)
        last = pltpu.roll(packed, 32, 1)
        unit_row = last[0:1]
        mass_all = last[0:1, vectors : vectors + 1]
        along = gram[:, vectors : vectors + 1] / mass_all
        return gram, unit_row, along

    def inverse_factor(gram, unit_row, along):
        work = jnp.where(lane < vectors, gram - along * unit_row, 0.0)
        work = jnp.where(lane == line + 32, 1.0, work)
        for j in range(vectors):
            top = work[j : j + 1]
            ratio = work[:, j : j + 1] / top[:, j : j + 1]
            work = work - jnp.where(line[:, 0:1] > j, ratio, 0.0) * top
        diag = jnp.sum(jnp.where(lane == line, work, 0.0), axis=1, keepdims=True)
        work = work * (1.0 / jnp.sqrt(diag))
        return jnp.where(lane < vectors, pltpu.roll(work, 96, 1), 0.0)

    def mix(factor, value):
        padded = jnp.concatenate([value, jnp.zeros((128 - vectors, tlen), F32)], axis=0)
        return lax.dot_general(factor, padded, NN, precision=HIGH, preferred_element_type=F32)

    for b in range(rows):
        zext[0:vectors, b * tlen : (b + 1) * tlen] = v_win[2 * rows + b]
    reduce_send(0, 0, gram_packed())

    def left_side(value):
        hi, lo = split(value)
        return jnp.concatenate(
            [
                jnp.concatenate([hi, hi], axis=1),
                jnp.concatenate([lo, jnp.zeros_like(lo)], axis=1),
            ],
            axis=0,
        ).astype(BF16)

    def forward(step):
        used = 2 * half if step == 0 else 2 * vectors

        @pl.loop(0, slots, unroll=16)
        def _(s):
            left = lhs_win[tab[col_at + s], 0:used]
            both = lax.dot_general(left, t_flip[s], NN, preferred_element_type=F32)
            prod[s, 0:vectors] = both[0:vectors] + both[vectors : 2 * vectors]
            if step == 0:
                prod[s, vectors:] = both[2 * vectors : 2 * vectors + 8]

    def row_total(r, step):
        at = rmap_at + r * MOST_ROW
        used = half if step == 0 else vectors
        total = prod[tab[at], 0:used]
        for p in range(1, MOST_ROW):
            total = total + prod[tab[at + p], 0:used]
        if step == 0:
            row_inv[r] = 1.0 / total[vectors:]
        return total[0:vectors] * row_inv[r, 0:1]

    def backward(step):
        @pl.loop(0, slots, unroll=16)
        def _(s):
            left = lhs_row[tab[row_at + s]]
            both = lax.dot_general(left, t_own[s], NN, preferred_element_type=F32)
            prod[s, 0:vectors] = both[0:vectors] + both[vectors:]

        @pl.loop(0, win)
        def _(c):
            at = cmap_at + c * rows
            total = prod[tab[at], 0:vectors]
            for r in range(1, rows):
                total = total + prod[tab[at + r], 0:vectors]
            z_part[step, c] = total

    def exchange_z(step):
        def source(d):
            return z_part.at[step, pl.ds((2 + d) * rows, rows)]

        def target(d):
            return z_in.at[step, OFFSETS.index(d)]

        send(3 + step, source, target)
        finish(3 + step, source, target)
        z_own[...] = z_part[step, 2 * rows : 3 * rows]
        for i in range(4):
            @pl.when(valid[3 - i])
            def _(i=i):
                z_own[...] = z_own[...] + z_in[step, i]

    flip(slots // 2, slots)
    tail = lax.broadcasted_iota(jnp.int32, (16, 2 * tlen), 0)
    ones = jnp.where(tail < 8, 1.0, 0.0).astype(BF16)
    finish(0, own_v, to_v)
    finish(2, own_s, to_s)

    @pl.loop(0, win, unroll=4)
    def _(c):
        lhs_win[c, 0 : 2 * vectors] = left_side(v_win[c] * s_win[pl.ds(c, 1)])
        lhs_win[c, 2 * vectors :] = ones

    forward(0)
    reduce_send(0, 1, reduce_wait(0, 0))

    @pl.loop(0, rows)
    def _(r):
        lhs_row[r] = left_side(row_total(r, 0))

    backward(0)
    _, _, along = unpack(reduce_wait(0, 1))
    exchange_z(0)
    for b in range(rows):
        cleaned = z_own[b] * col_scale[b : b + 1] - along * root[b : b + 1]
        zext[0:vectors, b * tlen : (b + 1) * tlen] = cleaned
        v_win2[2 * rows + b] = cleaned * col_scale[b : b + 1]
    send(5, own_v2, to_v2)
    reduce_send(1, 0, gram_packed())
    finish(5, own_v2, to_v2)

    @pl.loop(0, win, unroll=4)
    def _(c):
        lhs_win[c, 0 : 2 * vectors] = left_side(v_win2[c])

    reduce_send(1, 1, reduce_wait(1, 0))
    forward(1)
    factor = inverse_factor(*unpack(reduce_wait(1, 1)))

    @pl.loop(0, rows)
    def _(r):
        lhs_row[r] = left_side(mix(factor, row_total(r, 1)))

    backward(1)
    exchange_z(1)
    for b in range(rows):
        zext[0:vectors, b * tlen : (b + 1) * tlen] = z_own[b] * col_scale[b : b + 1]
    reduce_send(2, 0, gram_packed())
    reduce_send(2, 1, reduce_wait(2, 0))
    gram, unit_row, along = unpack(reduce_wait(2, 1))
    factor = inverse_factor(gram, unit_row, along)
    factor = factor * math.sqrt(count * rows * tlen)
    for b in range(rows):
        cols = slice(b * tlen, (b + 1) * tlen)
        out[:, cols] = mix(factor, zext[0:vectors, cols] - along * root[b : b + 1])


def table_kernel(slots, rows, tile_row, tile_col, row_count, tab):
    first = lax.axis_index("rows") * rows
    win = 5 * rows
    cmap_at = 2 * slots
    rmap_at = cmap_at + win * rows

    @pl.loop(0, win * rows, unroll=16)
    def _(i):
        tab[cmap_at + i] = slots

    start = jnp.int32(0)
    for r in range(rows):
        size = row_count[r]
        for p in range(MOST_ROW):
            tab[rmap_at + r * MOST_ROW + p] = jnp.where(p < size, start + p, slots)
        start = start + size

    @pl.loop(0, slots, unroll=8)
    def _(s):
        tab[s] = tile_col[s] - (first - 2 * rows)
        tab[slots + s] = tile_row[s] - first

    @pl.loop(0, start)
    def _(s):
        tab[cmap_at + tab[s] * rows + tab[slots + s]] = s


def body(tile_values, tile_row, tile_col, row_count, start_basis):
    slots, tlen = tile_values.shape[:2]
    rows = row_count.shape[0]
    vectors = start_basis.shape[0]
    count = lax.axis_size("rows")
    near = 4 if count <= 16 else 8
    win = 5 * rows
    smem = pl.BlockSpec(memory_space=pltpu.SMEM)
    table = pl.pallas_call(
        functools.partial(table_kernel, slots, rows),
        out_shape=jax.ShapeDtypeStruct((2 * slots + win * rows + rows * MOST_ROW,), jnp.int32),
        in_specs=[smem] * 3,
        out_specs=smem,
    )(tile_row, tile_col, row_count)
    chunks = 8
    most = max(near, count // near)
    half = vectors + 8
    vmem = pltpu.VMEM
    return pl.pallas_call(
        functools.partial(kernel, count, near, slots, rows, vectors, tlen, chunks),
        out_shape=jax.ShapeDtypeStruct(start_basis.shape, F32),
        in_specs=[
            pl.BlockSpec(memory_space=pltpu.SMEM),
            pl.BlockSpec(memory_space=pltpu.VMEM),
            pl.BlockSpec(memory_space=pl.ANY),
        ],
        out_specs=pl.BlockSpec(memory_space=pltpu.VMEM),
        scratch_shapes=[
            vmem((slots, tlen, tlen), F32),
            vmem((slots, 2 * tlen, tlen), BF16),
            vmem((slots, 2 * tlen, tlen), BF16),
            vmem((slots + 1, 8, tlen), F32),
            vmem((slots + 1, half, tlen), F32),
            vmem((win, vectors, tlen), F32),
            vmem((win, vectors, tlen), F32),
            vmem((win, tlen), F32),
            vmem((win, 2 * half, 2 * tlen), BF16),
            vmem((rows, 2 * vectors, 2 * tlen), BF16),
            vmem((rows, 8, tlen), F32),
            vmem((5, rows, tlen), F32),
            vmem((4, rows, tlen), F32),
            vmem((2, win, vectors, tlen), F32),
            vmem((2, 4, rows, vectors, tlen), F32),
            vmem((rows, vectors, tlen), F32),
            vmem((128, rows * tlen), F32),
            vmem((3, 2, 8, 128), F32),
            vmem((3, 2, most, 8, 128), F32),
            pltpu.SemaphoreType.DMA((chunks,)),
            pltpu.SemaphoreType.DMA((6, 4)),
            pltpu.SemaphoreType.DMA((6, 4)),
            pltpu.SemaphoreType.DMA((3, 2, most)),
            pltpu.SemaphoreType.DMA((3, 2, most)),
        ],
        compiler_params=pltpu.CompilerParams(
            collective_id=0, has_side_effects=True, vmem_limit_bytes=56 * 1024 * 1024
        ),
    )(table, start_basis, tile_values)


def solution(mesh):
    placed = (
        P(("groups", "rows"), None, None),
        P(("groups", "rows")),
        P(("groups", "rows")),
        P(("groups", "rows")),
        P(None, ("groups", "rows")),
    )
    return jax.shard_map(
        body, mesh=mesh, in_specs=placed, out_specs=P(None, ("groups", "rows")), check_vma=False
    )
```

```python
import functools
import math

import jax
import jax.numpy as jnp
from jax import lax
from jax.experimental import pallas as pl
from jax.experimental.pallas import tpu as pltpu
from jax.sharding import PartitionSpec as P

MOST_ROW = 24
MESH = pl.DeviceIdType.MESH
OFFSETS = (-2, -1, 1, 2)
HIGH = lax.Precision.HIGHEST
NT = (((1,), (1,)), ((), ()))
NN = (((1,), (0,)), ((), ()))
F32 = jnp.float32
BF16 = jnp.bfloat16


def split(value):
    hi = value.astype(BF16).astype(F32)
    return hi, value - hi


def kernel(
    count, near, slots, rows, vectors, tlen, chunks,
    tab, basis, tiles_hbm, out,
    tiles, t_own, t_flip, c_part, prod, v_win, v_win2, s_win, lhs_win, lhs_row,
    row_inv, colw, col_in, z_part, z_in, z_own, zext, ar_out, ar_in,
    tile_sem, x_send, x_recv, a_send, a_recv,
):
    me = lax.axis_index("rows")
    far = count // near
    win = 5 * rows
    half = vectors + 8
    col_at, row_at = 0, slots
    cmap_at = 2 * slots
    rmap_at = cmap_at + win * rows
    per = slots // chunks

    tile_copies = []
    for c in range(chunks):
        part = pl.ds(c * per, per)
        copy = pltpu.make_async_copy(tiles_hbm.at[part], tiles.at[part], tile_sem.at[c])
        copy.start()
        tile_copies.append(copy)

    valid = [jnp.logical_and(me + d >= 0, me + d < count) for d in OFFSETS]
    stage_pos = (me % near, me // near)
    stage_len = (near, far)

    def partner(stage, j):
        if stage == 0:
            return (me // near) * near + (me % near + j) % near
        return ((me // near + j) % far) * near + me % near

    barrier = pltpu.get_barrier_semaphore()
    greeted = jnp.int32(near - 1 + far - 1)
    for d, ok in zip(OFFSETS, valid):
        greeted = greeted + ok.astype(jnp.int32)

        @pl.when(ok)
        def _(d=d):
            pl.semaphore_signal(barrier, inc=1, device_id={"rows": me + d}, device_id_type=MESH)

    for stage in (0, 1):
        for j in range(1, stage_len[stage]):
            pl.semaphore_signal(
                barrier, inc=1, device_id={"rows": partner(stage, j)}, device_id_type=MESH
            )

    for b in range(rows):
        v_win[2 * rows + b] = basis[:, b * tlen : (b + 1) * tlen]
    c_part[slots] = jnp.zeros((8, tlen), F32)
    prod[slots] = jnp.zeros((half, tlen), F32)
    zext[...] = jnp.zeros_like(zext)

    def neighbour(which, i, source, target):
        return pltpu.make_async_remote_copy(
            src_ref=source(OFFSETS[i]),
            dst_ref=target(OFFSETS[i]),
            send_sem=x_send.at[which, i],
            recv_sem=x_recv.at[which, i],
            device_id={"rows": me + OFFSETS[i]},
            device_id_type=MESH,
        )

    def send(which, source, target):
        for i in (0, 3, 1, 2):
            @pl.when(valid[i])
            def _(i=i):
                neighbour(which, i, source, target).start()

    def finish(which, source, target):
        for i in range(4):
            @pl.when(valid[i])
            def _(i=i):
                neighbour(which, i, source, target).wait_send()

            @pl.when(valid[3 - i])
            def _(i=i):
                neighbour(which, i, source, target).wait_recv()

    core = me % 2
    mate = me + 1 - 2 * core
    left_ok, right_ok = valid[0], valid[3]
    first_core = core == 0
    second_core = core == 1

    def piece(which, i, source, target, device):
        return pltpu.make_async_remote_copy(
            src_ref=source,
            dst_ref=target,
            send_sem=x_send.at[which, i],
            recv_sem=x_recv.at[which, i],
            device_id={"rows": device},
            device_id_type=MESH,
        )

    def halo(which, buf):
        def block(index):
            return buf.at[pl.ds(index * rows, rows)]

        down = piece(which, 0, block(2), block(4), me - 2)
        up = piece(which, 3, block(2), block(0), me + 2)
        across = piece(which, 1, block(2), block(1 + 2 * core), mate)
        onward = piece(which, 2, block(4 - 4 * core), block(3 - 2 * core), mate)
        return down, up, across, onward

    def halo_send(which, buf):
        down, up, across, _ = halo(which, buf)
        pl.when(left_ok)(down.start)
        pl.when(right_ok)(up.start)
        across.start()

    def halo_finish(which, buf):
        down, up, across, onward = halo(which, buf)

        @pl.when(jnp.logical_and(first_core, right_ok))
        def _():
            down.wait_recv()
            onward.start()

        @pl.when(jnp.logical_and(second_core, left_ok))
        def _():
            up.wait_recv()
            onward.start()

        pl.when(jnp.logical_and(second_core, right_ok))(down.wait_recv)
        pl.when(jnp.logical_and(first_core, left_ok))(up.wait_recv)
        across.wait_send()
        across.wait_recv()
        pl.when(left_ok)(down.wait_send)
        pl.when(right_ok)(up.wait_send)
        pl.when(jnp.logical_and(first_core, right_ok))(onward.wait_send)
        pl.when(jnp.logical_and(second_core, left_ok))(onward.wait_send)
        pl.when(jnp.logical_and(first_core, left_ok))(onward.wait_recv)
        pl.when(jnp.logical_and(second_core, right_ok))(onward.wait_recv)

    def own_s(d):
        return s_win.at[pl.ds(2 * rows, rows)]

    def to_s(d):
        return s_win.at[pl.ds((2 - d) * rows, rows)]

    def part_c(d):
        return colw.at[2 + d]

    def to_c(d):
        return col_in.at[OFFSETS.index(d)]

    def mass_chunk(c):
        tile_copies[c].wait()

        @pl.loop(c * per, (c + 1) * per, unroll=4)
        def _(s):
            tile = tiles[s]
            hi = tile.astype(BF16)
            t_own[s, 0:tlen] = hi
            t_own[s, tlen:] = (tile - hi.astype(F32)).astype(BF16)
            c_part[s] = jnp.sum(tile.reshape(tlen // 8, 8, tlen), axis=0)

    mass_chunk(0)
    pl.semaphore_wait(barrier, greeted)
    halo_send(0, v_win)
    for c in range(1, chunks):
        mass_chunk(c)

    @pl.loop(0, 5)
    def _(w):
        lines = []
        for b in range(rows):
            at = cmap_at + (w * rows + b) * rows
            total = c_part[tab[at]]
            for r in range(1, rows):
                total = total + c_part[tab[at + r]]
            lines.append(jnp.sum(total, axis=0, keepdims=True))
        colw[w] = jnp.concatenate(lines, axis=0)

    def flip(begin, end):
        @pl.loop(begin, end, unroll=4)
        def _(s):
            t_flip[s, 0:tlen] = t_own[s, 0:tlen].T
            t_flip[s, tlen:] = t_own[s, tlen:].T

    send(1, part_c, to_c)
    flip(0, slots // 2)
    finish(1, part_c, to_c)
    for i in range(4):
        @pl.when(valid[3 - i])
        def _(i=i):
            colw[2] = colw[2] + col_in[i]

    mass = colw[2]
    col_scale = 1.0 / jnp.sqrt(mass)
    root = jnp.sqrt(mass)
    s_win[2 * rows : 3 * rows] = col_scale
    send(2, own_s, to_s)

    for b in range(rows):
        zext[vectors : vectors + 1, b * tlen : (b + 1) * tlen] = root[b : b + 1]

    def reduce_copy(which, stage, j):
        return pltpu.make_async_remote_copy(
            src_ref=ar_out.at[which, stage],
            dst_ref=ar_in.at[which, stage, j - 1],
            send_sem=a_send.at[which, stage, j - 1],
            recv_sem=a_recv.at[which, stage, j - 1],
            device_id={"rows": partner(stage, j)},
            device_id_type=MESH,
        )

    def reduce_send(which, stage, value):
        ar_out[which, stage] = value
        for j in range(1, stage_len[stage]):
            reduce_copy(which, stage, j).start()

    def reduce_wait(which, stage):
        total = ar_out[which, stage]
        for j in range(1, stage_len[stage]):
            copy = reduce_copy(which, stage, j)
            copy.wait_send()
            copy.wait_recv()
            total = total + ar_in[which, stage, j - 1]
        return total

    def gram_packed():
        value = zext[...]
        gram = lax.dot_general(value[0:32], value, NT, precision=HIGH, preferred_element_type=F32)
        packed = gram[0:8]
        for b in range(1, 4):
            packed = packed + pltpu.roll(gram[8 * b : 8 * b + 8], 32 * b, 1)
        return packed

    lane = lax.broadcasted_iota(jnp.int32, (vectors, 128), 1)
    line = lax.broadcasted_iota(jnp.int32, (vectors, 128), 0)

    def unpack(packed):
        parts = [packed] + [pltpu.roll(packed, 128 - 32 * b, 1) for b in (1, 2)]
        gram = jnp.concatenate(parts, axis=0)
        last = pltpu.roll(packed, 32, 1)
        unit_row = last[0:1]
        mass_all = last[0:1, vectors : vectors + 1]
        along = gram[:, vectors : vectors + 1] / mass_all
        return gram, unit_row, along

    def inverse_factor(gram, unit_row, along):
        work = jnp.where(lane < vectors, gram - along * unit_row, 0.0)
        work = jnp.where(lane == line + 32, 1.0, work)
        for j in range(vectors):
            top = work[j : j + 1]
            ratio = work[:, j : j + 1] / top[:, j : j + 1]
            work = work - jnp.where(line[:, 0:1] > j, ratio, 0.0) * top
        diag = jnp.sum(jnp.where(lane == line, work, 0.0), axis=1, keepdims=True)
        work = work * (1.0 / jnp.sqrt(diag))
        return jnp.where(lane < vectors, pltpu.roll(work, 96, 1), 0.0)

    def mix(factor, value):
        padded = jnp.concatenate([value, jnp.zeros((128 - vectors, tlen), F32)], axis=0)
        return lax.dot_general(factor, padded, NN, precision=HIGH, preferred_element_type=F32)

    for b in range(rows):
        zext[0:vectors, b * tlen : (b + 1) * tlen] = v_win[2 * rows + b]
    reduce_send(0, 0, gram_packed())

    def left_side(value):
        hi, lo = split(value)
        return jnp.concatenate(
            [
                jnp.concatenate([hi, hi], axis=1),
                jnp.concatenate([lo, jnp.zeros_like(lo)], axis=1),
            ],
            axis=0,
        ).astype(BF16)

    def forward(step):
        used = 2 * half if step == 0 else 2 * vectors

        @pl.loop(0, slots, unroll=32)
        def _(s):
            left = lhs_win[tab[col_at + s], 0:used]
            both = lax.dot_general(left, t_flip[s], NN, preferred_element_type=F32)
            prod[s, 0:vectors] = both[0:vectors] + both[vectors : 2 * vectors]
            if step == 0:
                prod[s, vectors:] = both[2 * vectors : 2 * vectors + 8]

    def row_total(r, step):
        at = rmap_at + r * MOST_ROW
        used = half if step == 0 else vectors
        total = prod[tab[at], 0:used]
        for p in range(1, MOST_ROW):
            total = total + prod[tab[at + p], 0:used]
        if step == 0:
            row_inv[r] = 1.0 / total[vectors:]
        return total[0:vectors] * row_inv[r, 0:1]

    def backward(step):
        @pl.loop(0, slots, unroll=32)
        def _(s):
            left = lhs_row[tab[row_at + s]]
            both = lax.dot_general(left, t_own[s], NN, preferred_element_type=F32)
            prod[s, 0:vectors] = both[0:vectors] + both[vectors:]

        @pl.loop(0, win, unroll=8)
        def _(c):
            at = cmap_at + c * rows
            total = prod[tab[at], 0:vectors]
            for r in range(1, rows):
                total = total + prod[tab[at + r], 0:vectors]
            z_part[step, c] = total

    def exchange_z(step):
        def window(index):
            return z_part.at[step, pl.ds(index * rows, rows)]

        which = 3 + step
        joined = piece(which, 1, window(1 + 2 * core), z_in.at[step, 1], mate)
        across = piece(which, 2, window(3 - 2 * core), z_in.at[step, 2], mate)
        down = piece(which, 0, window(0), z_in.at[step, 0], me - 2)
        up = piece(which, 3, window(4), z_in.at[step, 3], me + 2)
        joined.start()
        pl.when(jnp.logical_and(first_core, left_ok))(down.start)
        pl.when(jnp.logical_and(second_core, right_ok))(up.start)
        across.start()
        joined.wait_send()
        joined.wait_recv()
        at = pl.ds((4 - 4 * core) * rows, rows)
        z_part[step, at] = z_part[step, at] + z_in[step, 1]
        pl.when(jnp.logical_and(first_core, right_ok))(up.start)
        pl.when(jnp.logical_and(second_core, left_ok))(down.start)
        across.wait_send()
        across.wait_recv()
        z_own[...] = z_part[step, 2 * rows : 3 * rows] + z_in[step, 2]

        @pl.when(right_ok)
        def _():
            down.wait_recv()
            z_own[...] = z_own[...] + z_in[step, 0]

        @pl.when(left_ok)
        def _():
            up.wait_recv()
            z_own[...] = z_own[...] + z_in[step, 3]

        pl.when(left_ok)(down.wait_send)
        pl.when(right_ok)(up.wait_send)

    flip(slots // 2, slots)
    tail = lax.broadcasted_iota(jnp.int32, (16, 2 * tlen), 0)
    ones = jnp.where(tail < 8, 1.0, 0.0).astype(BF16)
    halo_finish(0, v_win)
    finish(2, own_s, to_s)

    @pl.loop(0, win, unroll=4)
    def _(c):
        lhs_win[c, 0 : 2 * vectors] = left_side(v_win[c] * s_win[pl.ds(c, 1)])
        lhs_win[c, 2 * vectors :] = ones

    forward(0)
    reduce_send(0, 1, reduce_wait(0, 0))

    @pl.loop(0, rows, unroll=4)
    def _(r):
        lhs_row[r] = left_side(row_total(r, 0))

    backward(0)
    _, _, along = unpack(reduce_wait(0, 1))
    exchange_z(0)
    for b in range(rows):
        cleaned = z_own[b] * col_scale[b : b + 1] - along * root[b : b + 1]
        zext[0:vectors, b * tlen : (b + 1) * tlen] = cleaned
        v_win2[2 * rows + b] = cleaned * col_scale[b : b + 1]
    halo_send(5, v_win2)
    reduce_send(1, 0, gram_packed())
    halo_finish(5, v_win2)

    @pl.loop(0, win, unroll=4)
    def _(c):
        lhs_win[c, 0 : 2 * vectors] = left_side(v_win2[c])

    reduce_send(1, 1, reduce_wait(1, 0))
    forward(1)
    factor = inverse_factor(*unpack(reduce_wait(1, 1)))

    @pl.loop(0, rows, unroll=4)
    def _(r):
        lhs_row[r] = left_side(mix(factor, row_total(r, 1)))

    backward(1)
    exchange_z(1)
    for b in range(rows):
        zext[0:vectors, b * tlen : (b + 1) * tlen] = z_own[b] * col_scale[b : b + 1]
    reduce_send(2, 0, gram_packed())
    reduce_send(2, 1, reduce_wait(2, 0))
    gram, unit_row, along = unpack(reduce_wait(2, 1))
    factor = inverse_factor(gram, unit_row, along)
    factor = factor * math.sqrt(count * rows * tlen)
    for b in range(rows):
        cols = slice(b * tlen, (b + 1) * tlen)
        out[:, cols] = mix(factor, zext[0:vectors, cols] - along * root[b : b + 1])


def table_kernel(slots, rows, tile_row, tile_col, row_count, tab):
    first = lax.axis_index("rows") * rows
    win = 5 * rows
    cmap_at = 2 * slots
    rmap_at = cmap_at + win * rows

    @pl.loop(0, win * rows, unroll=16)
    def _(i):
        tab[cmap_at + i] = slots

    start = jnp.int32(0)
    for r in range(rows):
        size = row_count[r]
        for p in range(MOST_ROW):
            tab[rmap_at + r * MOST_ROW + p] = jnp.where(p < size, start + p, slots)
        start = start + size

    @pl.loop(0, slots, unroll=8)
    def _(s):
        tab[s] = tile_col[s] - (first - 2 * rows)
        tab[slots + s] = tile_row[s] - first

    @pl.loop(0, start)
    def _(s):
        tab[cmap_at + tab[s] * rows + tab[slots + s]] = s


def body(tile_values, tile_row, tile_col, row_count, start_basis):
    slots, tlen = tile_values.shape[:2]
    rows = row_count.shape[0]
    vectors = start_basis.shape[0]
    count = lax.axis_size("rows")
    near = 4 if count <= 16 else 8
    win = 5 * rows
    smem = pl.BlockSpec(memory_space=pltpu.SMEM)
    table = pl.pallas_call(
        functools.partial(table_kernel, slots, rows),
        out_shape=jax.ShapeDtypeStruct((2 * slots + win * rows + rows * MOST_ROW,), jnp.int32),
        in_specs=[smem] * 3,
        out_specs=smem,
    )(tile_row, tile_col, row_count)
    chunks = 8
    most = max(near, count // near)
    half = vectors + 8
    vmem = pltpu.VMEM
    return pl.pallas_call(
        functools.partial(kernel, count, near, slots, rows, vectors, tlen, chunks),
        out_shape=jax.ShapeDtypeStruct(start_basis.shape, F32),
        in_specs=[
            pl.BlockSpec(memory_space=pltpu.SMEM),
            pl.BlockSpec(memory_space=pltpu.VMEM),
            pl.BlockSpec(memory_space=pl.ANY),
        ],
        out_specs=pl.BlockSpec(memory_space=pltpu.VMEM),
        scratch_shapes=[
            vmem((slots, tlen, tlen), F32),
            vmem((slots, 2 * tlen, tlen), BF16),
            vmem((slots, 2 * tlen, tlen), BF16),
            vmem((slots + 1, 8, tlen), F32),
            vmem((slots + 1, half, tlen), F32),
            vmem((win, vectors, tlen), F32),
            vmem((win, vectors, tlen), F32),
            vmem((win, tlen), F32),
            vmem((win, 2 * half, 2 * tlen), BF16),
            vmem((rows, 2 * vectors, 2 * tlen), BF16),
            vmem((rows, 8, tlen), F32),
            vmem((5, rows, tlen), F32),
            vmem((4, rows, tlen), F32),
            vmem((2, win, vectors, tlen), F32),
            vmem((2, 4, rows, vectors, tlen), F32),
            vmem((rows, vectors, tlen), F32),
            vmem((128, rows * tlen), F32),
            vmem((3, 2, 8, 128), F32),
            vmem((3, 2, most, 8, 128), F32),
            pltpu.SemaphoreType.DMA((chunks,)),
            pltpu.SemaphoreType.DMA((6, 4)),
            pltpu.SemaphoreType.DMA((6, 4)),
            pltpu.SemaphoreType.DMA((3, 2, most)),
            pltpu.SemaphoreType.DMA((3, 2, most)),
        ],
        compiler_params=pltpu.CompilerParams(
            collective_id=0, has_side_effects=True, vmem_limit_bytes=56 * 1024 * 1024
        ),
    )(table, start_basis, tile_values)


def solution(mesh):
    placed = (
        P(("groups", "rows"), None, None),
        P(("groups", "rows")),
        P(("groups", "rows")),
        P(("groups", "rows")),
        P(None, ("groups", "rows")),
    )
    return jax.shard_map(
        body, mesh=mesh, in_specs=placed, out_specs=P(None, ("groups", "rows")), check_vma=False
    )
```

```python
import functools
import math

import jax
import jax.numpy as jnp
from jax import lax
from jax.experimental import pallas as pl
from jax.experimental.pallas import tpu as pltpu
from jax.sharding import PartitionSpec as P

MOST_ROW = 24
MESH = pl.DeviceIdType.MESH
OFFSETS = (-2, -1, 1, 2)
HIGH = lax.Precision.HIGHEST
NT = (((1,), (1,)), ((), ()))
NN = (((1,), (0,)), ((), ()))
F32 = jnp.float32
BF16 = jnp.bfloat16


def split(value):
    hi = value.astype(BF16).astype(F32)
    return hi, value - hi


def kernel(
    count, near, slots, rows, vectors, tlen, chunks,
    tab, basis, tiles_hbm, out,
    tiles, t_own, t_flip, c_part, prod, v_win, v_win2, s_win, lhs_win, lhs_row,
    row_inv, colw, col_in, z_part, z_in, z_own, zext, ar_out, ar_in,
    tile_sem, x_send, x_recv, a_send, a_recv,
):
    me = lax.axis_index("rows")
    far = count // near
    win = 5 * rows
    half = vectors + 8
    col_at, row_at = 0, slots
    cmap_at = 2 * slots
    rmap_at = cmap_at + win * rows
    per = slots // chunks

    tile_copies = []
    for c in range(chunks):
        part = pl.ds(c * per, per)
        copy = pltpu.make_async_copy(tiles_hbm.at[part], tiles.at[part], tile_sem.at[c])
        copy.start()
        tile_copies.append(copy)

    valid = [jnp.logical_and(me + d >= 0, me + d < count) for d in OFFSETS]
    stage_pos = (me % near, me // near)
    stage_len = (near, far)

    def partner(stage, j):
        if stage == 0:
            return (me // near) * near + (me % near + j) % near
        return ((me // near + j) % far) * near + me % near

    barrier = pltpu.get_barrier_semaphore()
    greeted = jnp.int32(near - 1 + far - 1)
    for d, ok in zip(OFFSETS, valid):
        greeted = greeted + ok.astype(jnp.int32)

        @pl.when(ok)
        def _(d=d):
            pl.semaphore_signal(barrier, inc=1, device_id={"rows": me + d}, device_id_type=MESH)

    for stage in (0, 1):
        for j in range(1, stage_len[stage]):
            pl.semaphore_signal(
                barrier, inc=1, device_id={"rows": partner(stage, j)}, device_id_type=MESH
            )

    for b in range(rows):
        v_win[2 * rows + b] = basis[:, b * tlen : (b + 1) * tlen]
    c_part[slots] = jnp.zeros((8, tlen), F32)
    prod[slots] = jnp.zeros((half, tlen), F32)
    zext[...] = jnp.zeros_like(zext)

    def neighbour(which, i, source, target):
        return pltpu.make_async_remote_copy(
            src_ref=source(OFFSETS[i]),
            dst_ref=target(OFFSETS[i]),
            send_sem=x_send.at[which, i],
            recv_sem=x_recv.at[which, i],
            device_id={"rows": me + OFFSETS[i]},
            device_id_type=MESH,
        )

    def send(which, source, target):
        for i in (0, 3, 1, 2):
            @pl.when(valid[i])
            def _(i=i):
                neighbour(which, i, source, target).start()

    def finish(which, source, target):
        for i in range(4):
            @pl.when(valid[i])
            def _(i=i):
                neighbour(which, i, source, target).wait_send()

            @pl.when(valid[3 - i])
            def _(i=i):
                neighbour(which, i, source, target).wait_recv()

    core = me % 2
    mate = me + 1 - 2 * core
    left_ok, right_ok = valid[0], valid[3]
    first_core = core == 0
    second_core = core == 1

    def piece(which, i, source, target, device):
        return pltpu.make_async_remote_copy(
            src_ref=source,
            dst_ref=target,
            send_sem=x_send.at[which, i],
            recv_sem=x_recv.at[which, i],
            device_id={"rows": device},
            device_id_type=MESH,
        )

    def halo(which, buf):
        def block(index):
            return buf.at[pl.ds(index * rows, rows)]

        down = piece(which, 0, block(2), block(4), me - 2)
        up = piece(which, 3, block(2), block(0), me + 2)
        across = piece(which, 1, block(2), block(1 + 2 * core), mate)
        onward = piece(which, 2, block(4 - 4 * core), block(3 - 2 * core), mate)
        return down, up, across, onward

    def halo_send(which, buf):
        down, up, across, _ = halo(which, buf)
        pl.when(left_ok)(down.start)
        pl.when(right_ok)(up.start)
        across.start()

    def halo_relay(which, buf):
        down, up, across, onward = halo(which, buf)

        @pl.when(jnp.logical_and(first_core, right_ok))
        def _():
            down.wait_recv()
            onward.start()

        @pl.when(jnp.logical_and(second_core, left_ok))
        def _():
            up.wait_recv()
            onward.start()

    def halo_finish(which, buf):
        down, up, across, onward = halo(which, buf)
        pl.when(jnp.logical_and(second_core, right_ok))(down.wait_recv)
        pl.when(jnp.logical_and(first_core, left_ok))(up.wait_recv)
        across.wait_send()
        across.wait_recv()
        pl.when(left_ok)(down.wait_send)
        pl.when(right_ok)(up.wait_send)
        pl.when(jnp.logical_and(first_core, right_ok))(onward.wait_send)
        pl.when(jnp.logical_and(second_core, left_ok))(onward.wait_send)
        pl.when(jnp.logical_and(first_core, left_ok))(onward.wait_recv)
        pl.when(jnp.logical_and(second_core, right_ok))(onward.wait_recv)

    def own_s(d):
        return s_win.at[pl.ds(2 * rows, rows)]

    def to_s(d):
        return s_win.at[pl.ds((2 - d) * rows, rows)]

    def part_c(d):
        return colw.at[2 + d]

    def to_c(d):
        return col_in.at[OFFSETS.index(d)]

    def mass_chunk(c):
        tile_copies[c].wait()

        @pl.loop(c * per, (c + 1) * per, unroll=4)
        def _(s):
            tile = tiles[s]
            hi = tile.astype(BF16)
            t_own[s, 0:tlen] = hi
            t_own[s, tlen:] = (tile - hi.astype(F32)).astype(BF16)
            c_part[s] = jnp.sum(tile.reshape(tlen // 8, 8, tlen), axis=0)

    mass_chunk(0)
    pl.semaphore_wait(barrier, greeted)
    halo_send(0, v_win)
    for c in range(1, chunks):
        mass_chunk(c)

    @pl.loop(0, 5)
    def _(w):
        lines = []
        for b in range(rows):
            at = cmap_at + (w * rows + b) * rows
            total = c_part[tab[at]]
            for r in range(1, rows):
                total = total + c_part[tab[at + r]]
            lines.append(jnp.sum(total, axis=0, keepdims=True))
        colw[w] = jnp.concatenate(lines, axis=0)

    def flip(begin, end):
        @pl.loop(begin, end, unroll=4)
        def _(s):
            t_flip[s, 0:tlen] = t_own[s, 0:tlen].T
            t_flip[s, tlen:] = t_own[s, tlen:].T

    send(1, part_c, to_c)
    flip(0, slots // 2)
    finish(1, part_c, to_c)
    for i in range(4):
        @pl.when(valid[3 - i])
        def _(i=i):
            colw[2] = colw[2] + col_in[i]

    mass = colw[2]
    col_scale = 1.0 / jnp.sqrt(mass)
    root = jnp.sqrt(mass)
    s_win[2 * rows : 3 * rows] = col_scale
    send(2, own_s, to_s)

    for b in range(rows):
        zext[vectors : vectors + 1, b * tlen : (b + 1) * tlen] = root[b : b + 1]

    def reduce_copy(which, stage, j):
        return pltpu.make_async_remote_copy(
            src_ref=ar_out.at[which, stage],
            dst_ref=ar_in.at[which, stage, j - 1],
            send_sem=a_send.at[which, stage, j - 1],
            recv_sem=a_recv.at[which, stage, j - 1],
            device_id={"rows": partner(stage, j)},
            device_id_type=MESH,
        )

    def reduce_send(which, stage, value):
        ar_out[which, stage] = value
        for j in range(1, stage_len[stage]):
            reduce_copy(which, stage, j).start()

    def reduce_wait(which, stage):
        total = ar_out[which, stage]
        for j in range(1, stage_len[stage]):
            copy = reduce_copy(which, stage, j)
            copy.wait_send()
            copy.wait_recv()
            total = total + ar_in[which, stage, j - 1]
        return total

    def gram_packed():
        value = zext[...]
        gram = lax.dot_general(value[0:32], value, NT, precision=HIGH, preferred_element_type=F32)
        packed = gram[0:8]
        for b in range(1, 4):
            packed = packed + pltpu.roll(gram[8 * b : 8 * b + 8], 32 * b, 1)
        return packed

    lane = lax.broadcasted_iota(jnp.int32, (vectors, 128), 1)
    line = lax.broadcasted_iota(jnp.int32, (vectors, 128), 0)

    def unpack(packed):
        parts = [packed] + [pltpu.roll(packed, 128 - 32 * b, 1) for b in (1, 2)]
        gram = jnp.concatenate(parts, axis=0)
        last = pltpu.roll(packed, 32, 1)
        unit_row = last[0:1]
        mass_all = last[0:1, vectors : vectors + 1]
        along = gram[:, vectors : vectors + 1] / mass_all
        return gram, unit_row, along

    def inverse_factor(gram, unit_row, along):
        work = jnp.where(lane < vectors, gram - along * unit_row, 0.0)
        work = jnp.where(lane == line + 32, 1.0, work)
        for j in range(vectors):
            top = work[j : j + 1]
            ratio = work[:, j : j + 1] / top[:, j : j + 1]
            work = work - jnp.where(line[:, 0:1] > j, ratio, 0.0) * top
        diag = jnp.sum(jnp.where(lane == line, work, 0.0), axis=1, keepdims=True)
        work = work * (1.0 / jnp.sqrt(diag))
        return jnp.where(lane < vectors, pltpu.roll(work, 96, 1), 0.0)

    def mix(factor, value):
        padded = jnp.concatenate([value, jnp.zeros((128 - vectors, tlen), F32)], axis=0)
        return lax.dot_general(factor, padded, NN, precision=HIGH, preferred_element_type=F32)

    for b in range(rows):
        zext[0:vectors, b * tlen : (b + 1) * tlen] = v_win[2 * rows + b]
    reduce_send(0, 0, gram_packed())

    def left_side(value):
        hi, lo = split(value)
        return jnp.concatenate(
            [
                jnp.concatenate([hi, hi], axis=1),
                jnp.concatenate([lo, jnp.zeros_like(lo)], axis=1),
            ],
            axis=0,
        ).astype(BF16)

    def forward(step):
        used = 2 * half if step == 0 else 2 * vectors

        @pl.loop(0, slots, unroll=32)
        def _(s):
            left = lhs_win[tab[col_at + s], 0:used]
            both = lax.dot_general(left, t_flip[s], NN, preferred_element_type=F32)
            prod[s, 0:vectors] = both[0:vectors] + both[vectors : 2 * vectors]
            if step == 0:
                prod[s, vectors:] = both[2 * vectors : 2 * vectors + 8]

    def row_total(r, step):
        at = rmap_at + r * MOST_ROW
        used = half if step == 0 else vectors
        total = prod[tab[at], 0:used]
        for p in range(1, MOST_ROW):
            total = total + prod[tab[at + p], 0:used]
        if step == 0:
            row_inv[r] = 1.0 / total[vectors:]
        return total[0:vectors] * row_inv[r, 0:1]

    def backward(step):
        @pl.loop(0, slots, unroll=32)
        def _(s):
            left = lhs_row[tab[row_at + s]]
            both = lax.dot_general(left, t_own[s], NN, preferred_element_type=F32)
            prod[s, 0:vectors] = both[0:vectors] + both[vectors:]

        @pl.loop(0, win, unroll=8)
        def _(c):
            at = cmap_at + c * rows
            total = prod[tab[at], 0:vectors]
            for r in range(1, rows):
                total = total + prod[tab[at + r], 0:vectors]
            z_part[step, c] = total

    def exchange_z(step):
        def window(index):
            return z_part.at[step, pl.ds(index * rows, rows)]

        which = 3 + step
        joined = piece(which, 1, window(1 + 2 * core), z_in.at[step, 1], mate)
        across = piece(which, 2, window(3 - 2 * core), z_in.at[step, 2], mate)
        down = piece(which, 0, window(0), z_in.at[step, 0], me - 2)
        up = piece(which, 3, window(4), z_in.at[step, 3], me + 2)
        joined.start()
        pl.when(jnp.logical_and(first_core, left_ok))(down.start)
        pl.when(jnp.logical_and(second_core, right_ok))(up.start)
        across.start()
        joined.wait_send()
        joined.wait_recv()
        at = pl.ds((4 - 4 * core) * rows, rows)
        z_part[step, at] = z_part[step, at] + z_in[step, 1]
        pl.when(jnp.logical_and(first_core, right_ok))(up.start)
        pl.when(jnp.logical_and(second_core, left_ok))(down.start)
        across.wait_send()
        across.wait_recv()
        z_own[...] = z_part[step, 2 * rows : 3 * rows] + z_in[step, 2]

        @pl.when(right_ok)
        def _():
            down.wait_recv()
            z_own[...] = z_own[...] + z_in[step, 0]

        @pl.when(left_ok)
        def _():
            up.wait_recv()
            z_own[...] = z_own[...] + z_in[step, 3]

        pl.when(left_ok)(down.wait_send)
        pl.when(right_ok)(up.wait_send)

    halo_relay(0, v_win)
    flip(slots // 2, slots)
    tail = lax.broadcasted_iota(jnp.int32, (16, 2 * tlen), 0)
    ones = jnp.where(tail < 8, 1.0, 0.0).astype(BF16)
    halo_finish(0, v_win)
    finish(2, own_s, to_s)

    @pl.loop(0, win, unroll=4)
    def _(c):
        lhs_win[c, 0 : 2 * vectors] = left_side(v_win[c] * s_win[pl.ds(c, 1)])
        lhs_win[c, 2 * vectors :] = ones

    forward(0)
    reduce_send(0, 1, reduce_wait(0, 0))

    @pl.loop(0, rows, unroll=4)
    def _(r):
        lhs_row[r] = left_side(row_total(r, 0))

    backward(0)
    _, _, along = unpack(reduce_wait(0, 1))
    exchange_z(0)
    for b in range(rows):
        cleaned = z_own[b] * col_scale[b : b + 1] - along * root[b : b + 1]
        zext[0:vectors, b * tlen : (b + 1) * tlen] = cleaned
        v_win2[2 * rows + b] = cleaned * col_scale[b : b + 1]
    halo_send(5, v_win2)
    reduce_send(1, 0, gram_packed())
    halo_relay(5, v_win2)
    halo_finish(5, v_win2)
    reduce_send(1, 1, reduce_wait(1, 0))

    @pl.loop(0, win, unroll=4)
    def _(c):
        lhs_win[c, 0 : 2 * vectors] = left_side(v_win2[c])

    forward(1)
    factor = inverse_factor(*unpack(reduce_wait(1, 1)))

    @pl.loop(0, rows, unroll=4)
    def _(r):
        lhs_row[r] = left_side(mix(factor, row_total(r, 1)))

    backward(1)
    exchange_z(1)
    for b in range(rows):
        zext[0:vectors, b * tlen : (b + 1) * tlen] = z_own[b] * col_scale[b : b + 1]
    reduce_send(2, 0, gram_packed())
    reduce_send(2, 1, reduce_wait(2, 0))
    gram, unit_row, along = unpack(reduce_wait(2, 1))
    factor = inverse_factor(gram, unit_row, along)
    factor = factor * math.sqrt(count * rows * tlen)
    for b in range(rows):
        cols = slice(b * tlen, (b + 1) * tlen)
        out[:, cols] = mix(factor, zext[0:vectors, cols] - along * root[b : b + 1])


def table_kernel(slots, rows, tile_row, tile_col, row_count, tab):
    first = lax.axis_index("rows") * rows
    win = 5 * rows
    cmap_at = 2 * slots
    rmap_at = cmap_at + win * rows

    @pl.loop(0, win * rows, unroll=16)
    def _(i):
        tab[cmap_at + i] = slots

    start = jnp.int32(0)
    for r in range(rows):
        size = row_count[r]
        for p in range(MOST_ROW):
            tab[rmap_at + r * MOST_ROW + p] = jnp.where(p < size, start + p, slots)
        start = start + size

    @pl.loop(0, slots, unroll=8)
    def _(s):
        tab[s] = tile_col[s] - (first - 2 * rows)
        tab[slots + s] = tile_row[s] - first

    @pl.loop(0, start)
    def _(s):
        tab[cmap_at + tab[s] * rows + tab[slots + s]] = s


def body(tile_values, tile_row, tile_col, row_count, start_basis):
    slots, tlen = tile_values.shape[:2]
    rows = row_count.shape[0]
    vectors = start_basis.shape[0]
    count = lax.axis_size("rows")
    near = count if count <= 16 else 8
    win = 5 * rows
    smem = pl.BlockSpec(memory_space=pltpu.SMEM)
    table = pl.pallas_call(
        functools.partial(table_kernel, slots, rows),
        out_shape=jax.ShapeDtypeStruct((2 * slots + win * rows + rows * MOST_ROW,), jnp.int32),
        in_specs=[smem] * 3,
        out_specs=smem,
    )(tile_row, tile_col, row_count)
    chunks = 8
    most = max(near, count // near)
    half = vectors + 8
    vmem = pltpu.VMEM
    return pl.pallas_call(
        functools.partial(kernel, count, near, slots, rows, vectors, tlen, chunks),
        out_shape=jax.ShapeDtypeStruct(start_basis.shape, F32),
        in_specs=[
            pl.BlockSpec(memory_space=pltpu.SMEM),
            pl.BlockSpec(memory_space=pltpu.VMEM),
            pl.BlockSpec(memory_space=pl.ANY),
        ],
        out_specs=pl.BlockSpec(memory_space=pltpu.VMEM),
        scratch_shapes=[
            vmem((slots, tlen, tlen), F32),
            vmem((slots, 2 * tlen, tlen), BF16),
            vmem((slots, 2 * tlen, tlen), BF16),
            vmem((slots + 1, 8, tlen), F32),
            vmem((slots + 1, half, tlen), F32),
            vmem((win, vectors, tlen), F32),
            vmem((win, vectors, tlen), F32),
            vmem((win, tlen), F32),
            vmem((win, 2 * half, 2 * tlen), BF16),
            vmem((rows, 2 * vectors, 2 * tlen), BF16),
            vmem((rows, 8, tlen), F32),
            vmem((5, rows, tlen), F32),
            vmem((4, rows, tlen), F32),
            vmem((2, win, vectors, tlen), F32),
            vmem((2, 4, rows, vectors, tlen), F32),
            vmem((rows, vectors, tlen), F32),
            vmem((128, rows * tlen), F32),
            vmem((3, 2, 8, 128), F32),
            vmem((3, 2, most, 8, 128), F32),
            pltpu.SemaphoreType.DMA((chunks,)),
            pltpu.SemaphoreType.DMA((6, 4)),
            pltpu.SemaphoreType.DMA((6, 4)),
            pltpu.SemaphoreType.DMA((3, 2, most)),
            pltpu.SemaphoreType.DMA((3, 2, most)),
        ],
        compiler_params=pltpu.CompilerParams(
            collective_id=0, has_side_effects=True, vmem_limit_bytes=56 * 1024 * 1024
        ),
    )(table, start_basis, tile_values)


def solution(mesh):
    placed = (
        P(("groups", "rows"), None, None),
        P(("groups", "rows")),
        P(("groups", "rows")),
        P(("groups", "rows")),
        P(None, ("groups", "rows")),
    )
    return jax.shard_map(
        body, mesh=mesh, in_specs=placed, out_specs=P(None, ("groups", "rows")), check_vma=False
    )
```
